32 devices in a mesh: row: 4 (over y, core), col: 8 (over z, x).
Axes of the slice: x: 2, y: 2, z: 4, core: 2. Of those that a mesh axis runs over, the one named last changes fastest.
Arguments:
- fock: bfloat16 [32768, 8, 4096], P('row', 'col'), may hold values from -6 to 6
- lmo_coef: bfloat16 [32768, 1024], P(('row', 'col')), may hold values from -0.078125 to 0.078125
- three_index: bfloat16 [32768, 512], P(('row', 'col')), may hold values from -6 to 6
- rotation: bfloat16 [8, 4, 1024, 512], P('col', 'row'), may hold values from -0.1875 to 0.1875
- lmo_ids: int32 [8, 4], replicated, may hold values from 0 to 31, as said below
- domains: int32 [32, 8], replicated, may hold values from -1 to 255, as said below
Outputs:
- proj_fock: float32 [8, 4, 512, 512], P('col', 'row')
- three_rot: bfloat16 [8, 4, 512, 512], P('col', 'row')
The draws below stay inside these ranges and needn't reach their ends.
Inputs may be any that keep to these rules, and one draw needn't show every extreme that they name: `lmo_ids`: every LMO number appears exactly once; row o lists the 4 LMOs owned by column set o. `domains`: entry k of a list is -1 or a block of row panel k // 2; entry 0 is never -1. The present blocks of one list lie in distinct column sets. For one owner o and one entry k, the blocks of the lists of lmo_ids[o, j] over all j lie in distinct column sets; for one j and one entry k, those of lmo_ids[o, j] over all o do too.
All inputs are finite; a program needn't handle non-finite values.
Results may differ from the reference program's by a relative error of at most 0.02.
Values may be sent and summed in bfloat16 or wider, within the bound.
A program may use at most 320 MiB of HBM per device.

```python
import jax
import jax.numpy as jnp
from jax import lax

N = 32768
NOCC = 1024
NAUXD = 512
NROT = 512
BLK = 128
DBLK = 8
NPAN = 4
NCS = 8
FR = 1024
BPD = 8
PB = 2
D = 1024
LMO_COL = 4
NLMO = 32


def domain_tables(key):
    subkeys = jax.random.split(jax.random.fold_in(key, 7), 6)
    slot_order = jax.random.permutation(subkeys[0], NLMO).astype(jnp.int32)
    shift_owner = jax.random.permutation(subkeys[1], NCS).astype(jnp.int32)
    shift_slot = jax.random.permutation(subkeys[2], NCS).astype(jnp.int32)[:LMO_COL]
    shift_entry = jax.random.permutation(subkeys[3], NCS).astype(jnp.int32)[:DBLK]
    col_set = (shift_owner[:, None, None] + shift_slot[None, :, None] + shift_entry[None, None, :]) % NCS
    panel_row = (jnp.arange(DBLK, dtype=jnp.int32) // PB)[None, None, :]
    sub_block = jax.random.randint(subkeys[4], (NCS, LMO_COL, DBLK), 0, BPD, dtype=jnp.int32)
    blocks = (panel_row * NCS + col_set) * BPD + sub_block
    present = jax.random.randint(subkeys[5], (NCS, LMO_COL, DBLK), 0, 4, dtype=jnp.int32) > 0
    present = present | (jnp.arange(DBLK, dtype=jnp.int32)[None, None, :] == 0)
    slot_doms = jnp.where(present, blocks, -1).astype(jnp.int32).reshape(NLMO, DBLK)
    domains = jnp.zeros((NLMO, DBLK), jnp.int32).at[slot_order].set(slot_doms)
    return (slot_order.reshape(NCS, LMO_COL), domains)


def draw_lmo_ids(key, part):
    return domain_tables(key)[0]


def draw_domains(key, part):
    return domain_tables(key)[1]


def shard_levels(key, dims, shards, low, largest):
    loudness = 1.0
    for dim, blocks in shards:
        steps = jax.random.uniform(jax.random.fold_in(jax.random.fold_in(key, 6), dim), (blocks,), jnp.float32, low / len(shards), largest / len(shards))
        loudness = loudness * jnp.repeat(jnp.exp(steps), dims[dim] // blocks).reshape((-1,) + (1,) * (len(dims) - 1 - dim))
    return loudness


def scatter_about(rng, shape, width, reach, cuts=(), kind=jnp.bfloat16):
    level = shard_levels(rng, shape, cuts, -0.22, 0.18) if cuts else 1.0
    array = jax.random.normal(rng, shape, jnp.float32) * width * level
    return jnp.minimum(jnp.maximum(array, -reach), reach).astype(kind)


def setup_inputs(seed: int = 0) -> dict:
    splits = jax.random.split(jax.random.key(seed), 7)
    return {
        "fock": scatter_about(splits[0], (N, NCS, N // NCS), 1.0, 6.0, ((0, 4), (1, 8))),
        "lmo_coef": scatter_about(splits[1], (N, NOCC), (6 * NOCC) ** -0.5, 0.078125, ((0, 32),)),
        "three_index": scatter_about(splits[2], (N, NAUXD), 1.0, 6.0, ((0, 32),)),
        "rotation": scatter_about(splits[3], (NCS, LMO_COL, D, NROT), D ** -0.5, 0.1875, ((0, 8), (1, 4))),
        "lmo_ids": draw_lmo_ids(jax.random.fold_in(splits[6], 71), 0),
        "domains": draw_domains(jax.random.fold_in(splits[6], 71), 0),
    }


def reference(fock, lmo_coef, three_index, rotation, lmo_ids, domains):
    coef_sets = lmo_coef.reshape(NPAN, NCS, FR, NOCC)

    def add_set(running, col_set):
        fock_cols = lax.dynamic_index_in_dim(fock, col_set, 1, keepdims=False)
        coef_rows = lax.dynamic_index_in_dim(coef_sets, col_set, 1, keepdims=False).reshape(NPAN * FR, NOCC)
        partial_value = jnp.dot(fock_cols, coef_rows, preferred_element_type=jnp.float32).astype(jnp.bfloat16)
        partial_value = lax.optimization_barrier(partial_value)
        return running + partial_value.astype(jnp.float32), None

    fock_coef, _ = lax.scan(add_set, jnp.zeros((N, NOCC), jnp.float32), jnp.arange(NCS, dtype=jnp.int32))
    occ_fock = jnp.dot(lmo_coef.T, fock_coef.astype(jnp.bfloat16), preferred_element_type=jnp.float32)
    correction = jnp.dot(lmo_coef, occ_fock.astype(jnp.bfloat16), preferred_element_type=jnp.float32)
    proj_rows = (fock_coef - 0.5 * correction).astype(jnp.bfloat16)
    all_rows = jnp.concatenate([lmo_coef, proj_rows, three_index], axis=1)
    slot_doms = jnp.take(domains, lmo_ids.reshape(-1), axis=0)
    slot_rots = rotation.reshape(NCS * LMO_COL, D, NROT)
    offsets = jnp.arange(BLK, dtype=jnp.int32)

    def finish(packed):
        slot_dom, slot_rot = packed
        present = slot_dom >= 0
        clipped = jnp.maximum(slot_dom, 0).astype(jnp.int32)
        row_index = (clipped[:, None] * BLK + offsets[None, :]).reshape(D).astype(jnp.int32)
        keep_rows = jnp.repeat(present, BLK, total_repeat_length=D)
        picked = jnp.take(all_rows, row_index, axis=0)
        picked = jnp.where(keep_rows[:, None], picked, jnp.zeros_like(picked))
        flat_dev = clipped // BPD
        col_set = jnp.repeat(flat_dev % NCS, BLK, total_repeat_length=D).astype(jnp.int32)
        col_base = (flat_dev // NCS) * FR + (clipped % BPD) * BLK
        col_pos = (jnp.repeat(col_base, BLK, total_repeat_length=D) + jnp.tile(offsets, DBLK)).astype(jnp.int32)
        fock_rows = jnp.take(fock, row_index, axis=0)
        domain_fock = fock_rows[:, col_set, col_pos]
        both_live = keep_rows[:, None] & keep_rows[None, :]
        domain_fock = jnp.where(both_live, domain_fock, jnp.zeros_like(domain_fock))
        coef_dom = picked[:, :NOCC]
        proj_dom = picked[:, NOCC:2 * NOCC]
        three_dom = picked[:, 2 * NOCC:]
        fock_half = jnp.dot(domain_fock, slot_rot, preferred_element_type=jnp.float32).astype(jnp.bfloat16)
        fock_rot = jnp.dot(slot_rot.T, fock_half, preferred_element_type=jnp.float32)
        coef_rot = jnp.dot(slot_rot.T, coef_dom, preferred_element_type=jnp.float32).astype(jnp.bfloat16)
        proj_rot = jnp.dot(slot_rot.T, proj_dom, preferred_element_type=jnp.float32).astype(jnp.bfloat16)
        result = fock_rot - jnp.dot(coef_rot, proj_rot.T, preferred_element_type=jnp.float32)
        result = result - jnp.dot(proj_rot, coef_rot.T, preferred_element_type=jnp.float32)
        three_out = jnp.dot(slot_rot.T, three_dom, preferred_element_type=jnp.float32).astype(jnp.bfloat16)
        return result, three_out

    proj_fock, three_rot = lax.map(finish, (slot_doms, slot_rots))
    return (proj_fock.reshape(NCS, LMO_COL, NROT, NROT), three_rot.reshape(NCS, LMO_COL, NROT, NAUXD))
```

```python
import functools

import jax
import jax.numpy as jnp
from jax import lax
from jax.experimental import pallas as pl
from jax.experimental.pallas import tpu as pltpu
from jax.sharding import PartitionSpec as P

BLK = 128


def pick_kernel(count, width, row_ref, col_ref, src_ref, out_ref, sems):
    def copy(i):
        rows = pl.ds(pl.multiple_of(row_ref[i] * BLK, BLK), BLK)
        cols = pl.ds(pl.multiple_of(col_ref[i] * width, BLK), width)
        return pltpu.make_async_copy(src_ref.at[rows, cols], out_ref.at[i], sems.at[i])

    @pl.loop(0, count)
    def _(i):
        copy(i).start()

    @pl.loop(0, count)
    def _(i):
        copy(i).wait()


def pick(src, rows, cols=None, width=None):
    rows = rows.reshape(-1).astype(jnp.int32)
    count = rows.shape[0]
    width = width or src.shape[1]
    cols = jnp.zeros_like(rows) if cols is None else cols.reshape(-1).astype(jnp.int32)
    return pl.pallas_call(
        functools.partial(pick_kernel, count, width),
        out_shape=jax.ShapeDtypeStruct((count, BLK, width), src.dtype),
        in_specs=[
            pl.BlockSpec(memory_space=pltpu.SMEM),
            pl.BlockSpec(memory_space=pltpu.SMEM),
            pl.BlockSpec(memory_space=pl.ANY),
        ],
        out_specs=pl.BlockSpec(memory_space=pltpu.VMEM),
        scratch_shapes=[pltpu.SemaphoreType.DMA((count,))],
        compiler_params=pltpu.CompilerParams(vmem_limit_bytes=16 << 20),
        cost_estimate=pl.CostEstimate(
            flops=0, bytes_accessed=2 * count * BLK * width * 2, transcendentals=0
        ),
    )(rows, cols, src)


def dot32(a, b):
    return jnp.dot(a, b, preferred_element_type=jnp.float32)


def swap(x, axis):
    return lax.all_to_all(x, axis, split_axis=0, concat_axis=0, tiled=True)


def reduce_sets(panel_fock, gathered, dev_rows, num_sets, my_col):
    if num_sets != 8:
        part = dot32(panel_fock, gathered).astype(jnp.bfloat16)
        return lax.psum_scatter(part, "col", scatter_dimension=0, tiled=True).astype(jnp.float32)
    zi, xi = my_col // 2, my_col % 2
    order = jnp.array([[3, 2, 1, 0], [3, 2, 0, 1], [0, 1, 3, 2], [0, 1, 2, 3]], jnp.int32)
    mine = lax.dynamic_index_in_dim(order, zi, 0, keepdims=False)
    pairs = [(c, c ^ 1) for c in range(8)]

    def part(dest_z, dest_x):
        rows = lax.dynamic_slice_in_dim(panel_fock, (dest_z * 2 + dest_x) * dev_rows, dev_rows, 0)
        return dot32(rows, gathered)

    sums = []
    for n in range(4):
        away = part(mine[n], 1 - xi).astype(jnp.bfloat16)
        came = lax.ppermute(away, "col", pairs)
        sums.append(part(mine[n], xi) + came.astype(jnp.float32))

    def hop(x, step, up):
        if up:
            perm = [(z * 2 + x_, z * 2 + 2 + x_) for z in range(step + 1) for x_ in range(2)]
        else:
            perm = [(z * 2 + x_, z * 2 - 2 + x_) for z in range(3 - step, 4) for x_ in range(2)]
        return lax.ppermute(x.astype(jnp.bfloat16), "col", perm).astype(jnp.float32)

    up = hop(sums[0], 0, True)
    down = hop(sums[0], 0, False)
    up = hop(jnp.where(zi == 0, sums[1], sums[0]) + up, 1, True)
    down = hop(jnp.where(zi == 3, sums[1], sums[0]) + down, 1, False)
    up_own = jnp.where(zi == 1, sums[1], sums[2])
    down_own = jnp.where(zi == 2, sums[1], sums[2])
    up = hop(up_own + up, 2, True)
    down = hop(down_own + down, 2, False)
    return sums[3] + up + down


def body(fock, lmo_coef, three_index, rotation, lmo_ids, domains):
    num_panels = lax.axis_size("row")
    num_sets = lax.axis_size("col")
    my_row = lax.axis_index("row")
    my_col = lax.axis_index("col")
    dev_rows = lmo_coef.shape[0]
    dev_blocks = dev_rows // BLK
    dom_blocks = domains.shape[1]
    per_panel = dom_blocks // num_panels
    dom_width = dom_blocks * BLK
    panel_fock = fock[:, 0, :]
    slot_rot = rotation[0, 0]

    lists = jnp.take(domains, lmo_ids, axis=0)
    present = lists >= 0
    clipped = jnp.maximum(lists, 0)
    flat_dev = clipped // dev_blocks
    col_set = flat_dev % num_sets
    panel_id = flat_dev // num_sets
    sub_block = clipped % dev_blocks
    col_tile = panel_id * dev_blocks + sub_block
    row_tile = col_set * dev_blocks + sub_block
    here = present & (col_set == my_col)

    def panel(x):
        return lax.dynamic_slice_in_dim(x, my_row * per_panel, per_panel, 2)

    row_pick = jnp.sum(jnp.where(panel(here), panel(sub_block), 0), axis=0)
    here_row = lax.dynamic_index_in_dim(here, my_row, 1, keepdims=False)
    tile_row = lax.dynamic_index_in_dim(col_tile, my_row, 1, keepdims=False)
    entry = jnp.arange(dom_blocks, dtype=jnp.int32)
    set_pick = jnp.sum(jnp.where(here_row, entry, 0), axis=1)
    coef_pick = jnp.sum(jnp.where(here_row, tile_row, 0), axis=1)
    my_col_tile = jnp.sum(jnp.where(here, col_tile, 0), axis=2)
    tile_rows = jnp.transpose(panel(row_tile), (1, 0, 2))
    tile_cols = jnp.broadcast_to(my_col_tile.T[:, :, None], tile_rows.shape)
    own_set = col_set[my_col, my_row]
    own_present = present[my_col, my_row]
    match = own_present & (own_set == jnp.arange(num_sets, dtype=jnp.int32)[:, None])
    own_entry = jnp.sum(jnp.where(match, entry, 0), axis=1)

    gathered = lax.all_gather(lmo_coef, "row", axis=0, tiled=True)

    tiles = pick(panel_fock, tile_rows, tile_cols, BLK)
    tiles = swap(tiles.reshape(num_panels, num_sets, per_panel, BLK, BLK), "row")
    tiles = jnp.transpose(tiles, (1, 0, 2, 3, 4)).reshape(num_sets, dom_blocks, BLK, BLK)
    tiles = swap(tiles, "col")

    three_rows = swap(pick(three_index, row_pick), "row")
    three_dom = swap(pick(three_rows.reshape(dom_width, -1), set_pick), "col")
    coef_dom = swap(pick(gathered, coef_pick), "col")

    fock_coef = reduce_sets(panel_fock, gathered, dev_rows, num_sets, my_col)
    coef_b = fock_coef.astype(jnp.bfloat16)

    occ_term = jnp.einsum("ri,rj->ij", lmo_coef, coef_b, preferred_element_type=jnp.float32)
    occ_part = lax.psum_scatter(occ_term, ("row", "col"), scatter_dimension=0, tiled=True)
    occ_b = lax.all_gather(occ_part.astype(jnp.bfloat16), ("row", "col"), axis=0, tiled=True)

    fc_rows = swap(pick(coef_b, row_pick), "row")
    fc_dom = swap(pick(fc_rows.reshape(dom_width, -1), set_pick), "col")

    rot_set = pick(slot_rot, own_entry)
    rot_set = jnp.where(jnp.any(match, axis=1)[:, None, None], rot_set, jnp.zeros_like(rot_set))
    rot_set = rot_set.reshape(num_sets * BLK, -1)
    rot_live = jnp.where(jnp.repeat(own_present, BLK)[:, None], slot_rot, jnp.zeros_like(slot_rot))

    def rotate(dom, rot):
        dom = dom.reshape(rot.shape[0], -1)
        return jnp.einsum("xm,xi->mi", rot, dom, preferred_element_type=jnp.float32)

    three_rot = rotate(three_dom, rot_set).astype(jnp.bfloat16)
    coef_rot = rotate(coef_dom, rot_set).astype(jnp.bfloat16)
    dom_fock = jnp.transpose(tiles, (1, 2, 0, 3)).reshape(dom_width, num_sets * BLK)
    fock_half = dot32(dom_fock, rot_set).astype(jnp.bfloat16)
    fock_rot = rotate(fock_half, rot_live)
    proj_rot = (rotate(fc_dom, rot_set) - 0.5 * dot32(coef_rot, occ_b)).astype(jnp.bfloat16)
    cross = jnp.einsum("mi,ni->mn", coef_rot, proj_rot, preferred_element_type=jnp.float32)
    proj_fock = fock_rot - cross - cross.T
    return (proj_fock[None, None], three_rot[None, None])


def solution(mesh):
    placed = (
        P("row", "col", None),
        P(("row", "col"), None),
        P(("row", "col"), None),
        P("col", "row", None, None),
        P(),
        P(),
    )
    return jax.shard_map(
        body,
        mesh=mesh,
        in_specs=placed,
        out_specs=(P("col", "row", None, None), P("col", "row", None, None)),
        check_vma=False,
    )
```

```python
import functools

import jax
import jax.numpy as jnp
from jax import lax
from jax.experimental import pallas as pl
from jax.experimental.pallas import tpu as pltpu
from jax.sharding import PartitionSpec as P

BLK = 128


def pick_kernel(count, width, row_ref, col_ref, src_ref, out_ref, sems):
    def copy(i):
        rows = pl.ds(pl.multiple_of(row_ref[i] * BLK, BLK), BLK)
        cols = pl.ds(pl.multiple_of(col_ref[i] * width, BLK), width)
        return pltpu.make_async_copy(src_ref.at[rows, cols], out_ref.at[i], sems.at[i])

    @pl.loop(0, count)
    def _(i):
        copy(i).start()

    @pl.loop(0, count)
    def _(i):
        copy(i).wait()


def pick(src, rows, cols=None, width=None):
    rows = rows.reshape(-1).astype(jnp.int32)
    count = rows.shape[0]
    width = width or src.shape[1]
    cols = jnp.zeros_like(rows) if cols is None else cols.reshape(-1).astype(jnp.int32)
    return pl.pallas_call(
        functools.partial(pick_kernel, count, width),
        out_shape=jax.ShapeDtypeStruct((count, BLK, width), src.dtype),
        in_specs=[
            pl.BlockSpec(memory_space=pltpu.SMEM),
            pl.BlockSpec(memory_space=pltpu.SMEM),
            pl.BlockSpec(memory_space=pl.ANY),
        ],
        out_specs=pl.BlockSpec(memory_space=pltpu.VMEM),
        scratch_shapes=[pltpu.SemaphoreType.DMA((count,))],
        compiler_params=pltpu.CompilerParams(vmem_limit_bytes=16 << 20),
        cost_estimate=pl.CostEstimate(
            flops=0, bytes_accessed=2 * count * BLK * width * 2, transcendentals=0
        ),
    )(rows, cols, src)


def dot32(a, b):
    return jnp.dot(a, b, preferred_element_type=jnp.float32)


def swap(x, axis):
    return lax.all_to_all(x, axis, split_axis=0, concat_axis=0, tiled=True)


def reduce_sets(panel_fock, gathered, beside, dev_rows, num_sets, my_col):
    if num_sets != 8:
        part = dot32(panel_fock, gathered).astype(jnp.bfloat16)
        return lax.psum_scatter(part, "col", scatter_dimension=0, tiled=True), beside
    zi, xi = my_col // 2, my_col % 2
    order = jnp.array([[3, 2, 1, 0], [3, 2, 0, 1], [0, 1, 3, 2], [0, 1, 2, 3]], jnp.int32)
    mine = lax.dynamic_index_in_dim(order, zi, 0, keepdims=False)
    pairs = [(c, c ^ 1) for c in range(8)]

    def part(dest_z, dest_x, gathered):
        rows = lax.dynamic_slice_in_dim(panel_fock, (dest_z * 2 + dest_x) * dev_rows, dev_rows, 0)
        return dot32(rows, gathered)

    away = [part(mine[n], 1 - xi, gathered).astype(jnp.bfloat16) for n in range(4)]
    came = [lax.ppermute(a, "col", pairs) for a in away]
    gathered, _ = lax.optimization_barrier((gathered, away[3]))
    sums = []
    for n in range(4):
        if n == 3:
            gathered, beside = lax.optimization_barrier((gathered, beside))
        total = part(mine[n], xi, gathered) + came[n].astype(jnp.float32)
        sums.append(total.astype(jnp.bfloat16))

    def hop(x, step, up):
        if up:
            perm = [(z * 2 + x_, z * 2 + 2 + x_) for z in range(step + 1) for x_ in range(2)]
        else:
            perm = [(z * 2 + x_, z * 2 - 2 + x_) for z in range(3 - step, 4) for x_ in range(2)]
        return lax.ppermute(x.astype(jnp.bfloat16), "col", perm).astype(jnp.float32)

    up = hop(sums[0], 0, True)
    down = hop(sums[0], 0, False)
    up = hop(jnp.where(zi == 0, sums[1], sums[0]) + up, 1, True)
    down = hop(jnp.where(zi == 3, sums[1], sums[0]) + down, 1, False)
    up_own = jnp.where(zi == 1, sums[1], sums[2])
    down_own = jnp.where(zi == 2, sums[1], sums[2])
    up = hop(up_own + up, 2, True)
    down = hop(down_own + down, 2, False)
    return (sums[3] + up + down).astype(jnp.bfloat16), beside


def body(fock, lmo_coef, three_index, rotation, lmo_ids, domains):
    num_panels = lax.axis_size("row")
    num_sets = lax.axis_size("col")
    my_row = lax.axis_index("row")
    my_col = lax.axis_index("col")
    dev_rows = lmo_coef.shape[0]
    dev_blocks = dev_rows // BLK
    dom_blocks = domains.shape[1]
    per_panel = dom_blocks // num_panels
    dom_width = dom_blocks * BLK
    panel_fock = fock[:, 0, :]
    slot_rot = rotation[0, 0]

    lists = jnp.take(domains, lmo_ids, axis=0)
    present = lists >= 0
    clipped = jnp.maximum(lists, 0)
    flat_dev = clipped // dev_blocks
    col_set = flat_dev % num_sets
    panel_id = flat_dev // num_sets
    sub_block = clipped % dev_blocks
    col_tile = panel_id * dev_blocks + sub_block
    row_tile = col_set * dev_blocks + sub_block
    here = present & (col_set == my_col)

    def panel(x):
        return lax.dynamic_slice_in_dim(x, my_row * per_panel, per_panel, 2)

    row_pick = jnp.sum(jnp.where(panel(here), panel(sub_block), 0), axis=0)
    here_row = lax.dynamic_index_in_dim(here, my_row, 1, keepdims=False)
    tile_row = lax.dynamic_index_in_dim(col_tile, my_row, 1, keepdims=False)
    entry = jnp.arange(dom_blocks, dtype=jnp.int32)
    set_pick = jnp.sum(jnp.where(here_row, entry, 0), axis=1)
    coef_pick = jnp.sum(jnp.where(here_row, tile_row, 0), axis=1)
    my_col_tile = jnp.sum(jnp.where(here, col_tile, 0), axis=2)
    tile_rows = jnp.transpose(panel(row_tile), (1, 0, 2))
    tile_cols = jnp.broadcast_to(my_col_tile.T[:, :, None], tile_rows.shape)
    own_set = col_set[my_col, my_row]
    own_present = present[my_col, my_row]
    match = own_present & (own_set == jnp.arange(num_sets, dtype=jnp.int32)[:, None])
    own_entry = jnp.sum(jnp.where(match, entry, 0), axis=1)

    gathered = lax.all_gather(lmo_coef, "row", axis=0, tiled=True)

    tiles = pick(panel_fock, tile_rows, tile_cols, BLK)
    tiles = swap(tiles.reshape(num_panels, num_sets, per_panel, BLK, BLK), "row")
    three_rows = swap(pick(three_index, row_pick), "row")
    gathered, tiles, three_rows = lax.optimization_barrier((gathered, tiles, three_rows))
    coef_dom = swap(pick(gathered, coef_pick), "col")
    tiles = jnp.transpose(tiles, (1, 0, 2, 3, 4)).reshape(num_sets, dom_blocks, BLK, BLK)
    tiles = swap(tiles, "col")
    three_dom = swap(pick(three_rows.reshape(dom_width, -1), set_pick), "col")

    coef_b, (coef_dom, tiles, three_dom) = reduce_sets(
        panel_fock, gathered, (coef_dom, tiles, three_dom), dev_rows, num_sets, my_col
    )

    occ_term = jnp.einsum("ri,rj->ij", lmo_coef, coef_b, preferred_element_type=jnp.float32)
    occ_term = occ_term.astype(jnp.bfloat16).reshape(num_panels, -1, occ_term.shape[1])
    fc_rows = pick(coef_b, row_pick).reshape(num_panels, per_panel * BLK, -1)
    both = swap(jnp.concatenate([occ_term, fc_rows], axis=1), "row")
    occ_rows = occ_term.shape[1]
    occ_part = jnp.sum(both[:, :occ_rows].astype(jnp.float32), axis=0).astype(jnp.bfloat16)
    fc_rows = both[:, occ_rows:].reshape(dom_width, -1)
    occ_part = swap(occ_part.reshape(num_sets, -1, occ_part.shape[1]), "col")
    occ_part = jnp.sum(occ_part.astype(jnp.float32), axis=0).astype(jnp.bfloat16)
    fc_dom = swap(pick(fc_rows, set_pick), "col")
    occ_part = swap(jnp.broadcast_to(occ_part, (num_sets, *occ_part.shape)), "col")
    occ_part = occ_part.reshape(occ_rows, -1)
    occ_pieces = [occ_part] + [
        lax.ppermute(occ_part, "row", [(p, (p + step) % num_panels) for p in range(num_panels)])
        for step in range(1, num_panels)
    ]

    rot_set = pick(slot_rot, own_entry)
    rot_set = jnp.where(jnp.any(match, axis=1)[:, None, None], rot_set, jnp.zeros_like(rot_set))
    rot_set = rot_set.reshape(num_sets * BLK, -1)
    rot_live = jnp.where(jnp.repeat(own_present, BLK)[:, None], slot_rot, jnp.zeros_like(slot_rot))

    def rotate(dom, rot):
        dom = dom.reshape(rot.shape[0], -1)
        return jnp.einsum("xm,xi->mi", rot, dom, preferred_element_type=jnp.float32)

    three_rot = rotate(three_dom, rot_set).astype(jnp.bfloat16)
    coef_rot = rotate(coef_dom, rot_set).astype(jnp.bfloat16)
    dom_fock = jnp.transpose(tiles, (1, 2, 0, 3)).reshape(dom_width, num_sets * BLK)
    fock_half = dot32(dom_fock, rot_set).astype(jnp.bfloat16)
    fock_rot = rotate(fock_half, rot_live)
    correction = 0.0
    for step, piece in enumerate(occ_pieces):
        start = (my_row - step) % num_panels * occ_rows
        coef_cols = lax.dynamic_slice_in_dim(coef_rot, start, occ_rows, 1)
        correction += dot32(coef_cols, piece)
    proj_rot = (rotate(fc_dom, rot_set) - 0.5 * correction).astype(jnp.bfloat16)
    cross = jnp.einsum("mi,ni->mn", coef_rot, proj_rot, preferred_element_type=jnp.float32)
    proj_fock = fock_rot - cross - cross.T
    return (proj_fock[None, None], three_rot[None, None])


def solution(mesh):
    placed = (
        P("row", "col", None),
        P(("row", "col"), None),
        P(("row", "col"), None),
        P("col", "row", None, None),
        P(),
        P(),
    )
    return jax.shard_map(
        body,
        mesh=mesh,
        in_specs=placed,
        out_specs=(P("col", "row", None, None), P("col", "row", None, None)),
        check_vma=False,
    )
```

```python
import functools

import jax
import jax.numpy as jnp
from jax import lax
from jax.experimental import pallas as pl
from jax.experimental.pallas import tpu as pltpu
from jax.sharding import PartitionSpec as P

BLK = 128


def pick_kernel(count, width, row_ref, col_ref, src_ref, out_ref, sems):
    def copy(i):
        rows = pl.ds(pl.multiple_of(row_ref[i] * BLK, BLK), BLK)
        cols = pl.ds(pl.multiple_of(col_ref[i] * width, BLK), width)
        return pltpu.make_async_copy(src_ref.at[rows, cols], out_ref.at[i], sems.at[i])

    @pl.loop(0, count)
    def _(i):
        copy(i).start()

    @pl.loop(0, count)
    def _(i):
        copy(i).wait()


def pick(src, rows, cols=None, width=None):
    rows = rows.reshape(-1).astype(jnp.int32)
    count = rows.shape[0]
    width = width or src.shape[1]
    cols = jnp.zeros_like(rows) if cols is None else cols.reshape(-1).astype(jnp.int32)
    return pl.pallas_call(
        functools.partial(pick_kernel, count, width),
        out_shape=jax.ShapeDtypeStruct((count, BLK, width), src.dtype),
        in_specs=[
            pl.BlockSpec(memory_space=pltpu.SMEM),
            pl.BlockSpec(memory_space=pltpu.SMEM),
            pl.BlockSpec(memory_space=pl.ANY),
        ],
        out_specs=pl.BlockSpec(memory_space=pltpu.VMEM),
        scratch_shapes=[pltpu.SemaphoreType.DMA((count,))],
        compiler_params=pltpu.CompilerParams(vmem_limit_bytes=16 << 20),
        cost_estimate=pl.CostEstimate(
            flops=0, bytes_accessed=2 * count * BLK * width * 2, transcendentals=0
        ),
    )(rows, cols, src)


def dot32(a, b):
    return jnp.dot(a, b, preferred_element_type=jnp.float32)


def swap(x, axis):
    return lax.all_to_all(x, axis, split_axis=0, concat_axis=0, tiled=True)


def reduce_sets(panel_fock, gathered, beside, dev_rows, num_sets, my_col):
    if num_sets != 8:
        part = dot32(panel_fock, gathered).astype(jnp.bfloat16)
        return lax.psum_scatter(part, "col", scatter_dimension=0, tiled=True), beside
    zi, xi = my_col // 2, my_col % 2
    order = jnp.array([[3, 2, 1, 0], [3, 2, 0, 1], [0, 1, 3, 2], [0, 1, 2, 3]], jnp.int32)
    mine = lax.dynamic_index_in_dim(order, zi, 0, keepdims=False)
    pairs = [(c, c ^ 1) for c in range(8)]

    def part(dest_z, dest_x, gathered):
        rows = lax.dynamic_slice_in_dim(panel_fock, (dest_z * 2 + dest_x) * dev_rows, dev_rows, 0)
        return dot32(rows, gathered)

    away = [part(mine[n], 1 - xi, gathered).astype(jnp.bfloat16) for n in range(4)]
    came = [lax.ppermute(a, "col", pairs) for a in away]
    gathered, _ = lax.optimization_barrier((gathered, away[3]))
    sums = []
    for n in range(4):
        total = part(mine[n], xi, gathered) + came[n].astype(jnp.float32)
        sums.append(total.astype(jnp.bfloat16))

    def hop(x, step, up):
        if up:
            perm = [(z * 2 + x_, z * 2 + 2 + x_) for z in range(step + 1) for x_ in range(2)]
        else:
            perm = [(z * 2 + x_, z * 2 - 2 + x_) for z in range(3 - step, 4) for x_ in range(2)]
        return lax.ppermute(x.astype(jnp.bfloat16), "col", perm).astype(jnp.float32)

    up = hop(sums[0], 0, True)
    down = hop(sums[0], 0, False)
    up = hop(jnp.where(zi == 0, sums[1], sums[0]) + up, 1, True)
    down = hop(jnp.where(zi == 3, sums[1], sums[0]) + down, 1, False)
    up_own = jnp.where(zi == 1, sums[1], sums[2])
    down_own = jnp.where(zi == 2, sums[1], sums[2])
    up = hop(up_own + up, 2, True)
    down = hop(down_own + down, 2, False)
    return (sums[3] + up + down).astype(jnp.bfloat16), beside


def body(fock, lmo_coef, three_index, rotation, lmo_ids, domains):
    num_panels = lax.axis_size("row")
    num_sets = lax.axis_size("col")
    my_row = lax.axis_index("row")
    my_col = lax.axis_index("col")
    dev_rows = lmo_coef.shape[0]
    dev_blocks = dev_rows // BLK
    dom_blocks = domains.shape[1]
    per_panel = dom_blocks // num_panels
    dom_width = dom_blocks * BLK
    panel_fock = fock[:, 0, :]
    slot_rot = rotation[0, 0]

    lists = jnp.take(domains, lmo_ids, axis=0)
    present = lists >= 0
    clipped = jnp.maximum(lists, 0)
    flat_dev = clipped // dev_blocks
    col_set = flat_dev % num_sets
    panel_id = flat_dev // num_sets
    sub_block = clipped % dev_blocks
    col_tile = panel_id * dev_blocks + sub_block
    row_tile = col_set * dev_blocks + sub_block
    here = present & (col_set == my_col)

    def panel(x):
        return lax.dynamic_slice_in_dim(x, my_row * per_panel, per_panel, 2)

    row_pick = jnp.sum(jnp.where(panel(here), panel(sub_block), 0), axis=0)
    here_row = lax.dynamic_index_in_dim(here, my_row, 1, keepdims=False)
    tile_row = lax.dynamic_index_in_dim(col_tile, my_row, 1, keepdims=False)
    entry = jnp.arange(dom_blocks, dtype=jnp.int32)
    set_pick = jnp.sum(jnp.where(here_row, entry, 0), axis=1)
    coef_pick = jnp.sum(jnp.where(here_row, tile_row, 0), axis=1)
    my_col_tile = jnp.sum(jnp.where(here, col_tile, 0), axis=2)
    tile_rows = jnp.transpose(panel(row_tile), (1, 0, 2))
    tile_cols = jnp.broadcast_to(my_col_tile.T[:, :, None], tile_rows.shape)
    own_set = col_set[my_col, my_row]
    own_present = present[my_col, my_row]
    match = own_present & (own_set == jnp.arange(num_sets, dtype=jnp.int32)[:, None])
    own_entry = jnp.sum(jnp.where(match, entry, 0), axis=1)

    gathered = lax.all_gather(lmo_coef, "row", axis=0, tiled=True)

    tiles = pick(panel_fock, tile_rows, tile_cols, BLK)
    tiles = swap(tiles.reshape(num_panels, num_sets, per_panel, BLK, BLK), "row")
    three_rows = swap(pick(three_index, row_pick), "row")
    coef_dom = swap(pick(gathered, coef_pick), "col")
    tiles = jnp.transpose(tiles, (1, 0, 2, 3, 4)).reshape(num_sets, dom_blocks, BLK, BLK)
    tiles = swap(tiles, "col")
    three_dom = swap(pick(three_rows.reshape(dom_width, -1), set_pick), "col")

    coef_b, (coef_dom, tiles, three_dom) = reduce_sets(
        panel_fock, gathered, (coef_dom, tiles, three_dom), dev_rows, num_sets, my_col
    )

    occ_term = jnp.einsum("ri,rj->ij", lmo_coef, coef_b, preferred_element_type=jnp.float32)
    occ_term = occ_term.astype(jnp.bfloat16).reshape(num_panels, -1, occ_term.shape[1])
    fc_rows = pick(coef_b, row_pick).reshape(num_panels, per_panel * BLK, -1)
    both = swap(jnp.concatenate([occ_term, fc_rows], axis=1), "row")
    occ_rows = occ_term.shape[1]
    occ_part = jnp.sum(both[:, :occ_rows].astype(jnp.float32), axis=0).astype(jnp.bfloat16)
    fc_rows = both[:, occ_rows:].reshape(dom_width, -1)
    occ_part = swap(occ_part.reshape(num_sets, -1, occ_part.shape[1]), "col")
    occ_part = jnp.sum(occ_part.astype(jnp.float32), axis=0).astype(jnp.bfloat16)
    fc_dom = swap(pick(fc_rows, set_pick), "col")
    occ_part = swap(jnp.broadcast_to(occ_part, (num_sets, *occ_part.shape)), "col")
    occ_part = occ_part.reshape(occ_rows, -1)
    occ_pieces = [occ_part] + [
        lax.ppermute(occ_part, "row", [(p, (p + step) % num_panels) for p in range(num_panels)])
        for step in range(1, num_panels)
    ]

    rot_set = pick(slot_rot, own_entry)
    rot_set = jnp.where(jnp.any(match, axis=1)[:, None, None], rot_set, jnp.zeros_like(rot_set))
    rot_set = rot_set.reshape(num_sets * BLK, -1)
    rot_live = jnp.where(jnp.repeat(own_present, BLK)[:, None], slot_rot, jnp.zeros_like(slot_rot))

    def rotate(dom, rot):
        dom = dom.reshape(rot.shape[0], -1)
        return jnp.einsum("xm,xi->mi", rot, dom, preferred_element_type=jnp.float32)

    three_rot = rotate(three_dom, rot_set).astype(jnp.bfloat16)
    coef_rot = rotate(coef_dom, rot_set).astype(jnp.bfloat16)
    dom_fock = jnp.transpose(tiles, (1, 2, 0, 3)).reshape(dom_width, num_sets * BLK)
    fock_half = dot32(dom_fock, rot_set).astype(jnp.bfloat16)
    fock_rot = rotate(fock_half, rot_live)
    correction = 0.0
    for step, piece in enumerate(occ_pieces):
        start = (my_row - step) % num_panels * occ_rows
        coef_cols = lax.dynamic_slice_in_dim(coef_rot, start, occ_rows, 1)
        correction += dot32(coef_cols, piece)
    proj_rot = (rotate(fc_dom, rot_set) - 0.5 * correction).astype(jnp.bfloat16)
    cross = jnp.einsum("mi,ni->mn", coef_rot, proj_rot, preferred_element_type=jnp.float32)
    proj_fock = fock_rot - cross - cross.T
    return (proj_fock[None, None], three_rot[None, None])


def solution(mesh):
    placed = (
        P("row", "col", None),
        P(("row", "col"), None),
        P(("row", "col"), None),
        P("col", "row", None, None),
        P(),
        P(),
    )
    return jax.shard_map(
        body,
        mesh=mesh,
        in_specs=placed,
        out_specs=(P("col", "row", None, None), P("col", "row", None, None)),
        check_vma=False,
    )
```
